256 devices in a mesh: spec: 32 (over x_lo, z, core), bucket: 8 (over y, x_hi).
Axes of the slice: x: 4 (x_hi: 2, x_lo: 2; x = x_hi * 2 + x_lo), y: 4, z: 8, core: 2. Of those that a mesh axis runs over, the one named last changes fastest.
Arguments:
- spectra: bfloat16 [2048, 65536], P('bucket', 'spec'), may hold values from 0 to 20
- theory: bfloat16 [512, 65536], P('bucket', 'spec'), may hold values from 0 to 16
- cand: int32 [2048, 128], P('bucket'), may hold values from 0 to 511
- half: int32 [128], P('spec'), may hold values from 25 to 75
Outputs:
- cand_scores: float32 [2048, 128], P('bucket')
- peptide_score: float32 [512], P(('spec', 'bucket'))
The draws below stay inside these ranges and needn't reach their ends.
All inputs are finite; a program needn't handle non-finite values.
Results may differ from the reference program's by a relative error of at most 0.0041.
Values may be sent and summed in bfloat16 or wider, within the bound.
No kernel may reach another device: no remote copies, remote signals or barrier semaphores. Data moves between devices by JAX's collectives and lax.ppermute only.
A program may use at most 64 MiB of HBM per device.

```python
import math
import jax
import jax.numpy as jnp
import numpy as np
from jax import lax

BINS = 65536
HALF = 75
REGION = 512
K = 128
SPEC_DEV = 256
NSPEC = 2048
PEPTIDES = 512
NREG = 128
LOAD = 512


def draw_spectra(key, part):
    key_scale, key_noise = jax.random.split(jax.random.fold_in(key, 101), 2)
    row_scale = jnp.exp(jax.random.uniform(key_scale, (NSPEC, 1), jnp.float32, 0.0, math.log(10.0)))
    uniform_noise = jax.random.uniform(key_noise, (NSPEC, BINS), jnp.float32)
    values = 2.0 * uniform_noise
    return (values * row_scale).astype(jnp.bfloat16)


def draw_theory(key, part):
    key_scale, key_noise = jax.random.split(jax.random.fold_in(key, 202), 2)
    uniform_noise = jax.random.uniform(key_noise, (PEPTIDES, BINS), jnp.float32)
    row_scale = jnp.exp(jax.random.uniform(key_scale, (PEPTIDES, 1), jnp.float32, 0.0, math.log(10.0)))
    values = uniform_noise
    return (values * row_scale).astype(jnp.bfloat16)


def with_ends(array, stream_key, smallest, largest):
    index_at = [jax.random.randint(jax.random.fold_in(stream_key, axis), (), 0, length) for axis, length in enumerate(array.shape)]
    longest = array.shape.index(max(array.shape))
    next_to = index_at[:longest] + [(index_at[longest] + 1) % array.shape[longest]] + index_at[longest + 1:]
    return array.at[tuple(index_at)].set(smallest).at[tuple(next_to)].set(largest)


def rank_table(count, lean):
    portions = [(1 << 20) // math.isqrt(grade ** lean) + 1 for grade in range(1, count + 1)]
    width = 1 + sum(portions) // (1 << 30)
    return np.cumsum(np.array([max(1, weight // width) for weight in portions]))


def skewed_ids(rng, extent, count, skew):
    grid = rank_table(count, skew)
    lot = jax.random.randint(jax.random.fold_in(rng, 1), extent, 0, int(grid[count - 1]))
    grade = jnp.searchsorted(jnp.asarray(grid, jnp.int32), lot, side="right")
    return jax.random.permutation(jax.random.fold_in(rng, 2), count)[grade].astype(jnp.int32)


def setup_inputs(seed: int = 0) -> dict:
    splits = jax.random.split(jax.random.key(seed), 5)
    spectra = draw_spectra(jax.random.fold_in(splits[4], 71), 0)
    theory = draw_theory(jax.random.fold_in(splits[4], 71), 0)
    cand = with_ends(skewed_ids(splits[2], (NSPEC, K), PEPTIDES, 1), jax.random.fold_in(splits[2], 3), 0, PEPTIDES - 1).astype(jnp.int32)
    half = with_ends(jax.random.randint(splits[3], (NREG,), HALF // 3, HALF + 1), jax.random.fold_in(splits[3], 1), HALF // 3, HALF).astype(jnp.int32)
    return {"spectra": spectra, "theory": theory, "cand": cand, "half": half}


def make_band(widths):
    block_iota = lax.broadcasted_iota(jnp.int32, (3, 128, 128), 0)
    input_iota = lax.broadcasted_iota(jnp.int32, (3, 128, 128), 1)
    output_iota = lax.broadcasted_iota(jnp.int32, (3, 128, 128), 2)
    offset = 128 * (block_iota - 1) + input_iota - output_iota
    return jnp.abs(offset)[None] <= widths[:, None, None, None]

def zscores(score_tile, cand_ids):
    average = lax.optimization_barrier(jnp.mean(score_tile, axis=1, keepdims=True))
    spread = lax.optimization_barrier(jnp.mean(jnp.square(score_tile - average), axis=1, keepdims=True))
    picked = jnp.take_along_axis(score_tile, cand_ids, axis=1)
    return (picked - average) * lax.rsqrt(spread + 1e-06)

def reference(spectra, theory, cand, half):
    tile_count = BINS // 128
    band_weights = make_band(jnp.repeat(half, REGION // 128)).astype(jnp.float32)
    bin_widths = jnp.repeat(half, REGION)
    divisor = (2 * bin_widths + 1).astype(jnp.float32)
    block_rows = min(SPEC_DEV, 512)

    def one_block(block_args):
        rows_in, cand_ids = block_args
        intensity = rows_in.astype(jnp.float32)
        extended = jnp.pad(intensity, ((0, 0), (128, 128))).reshape(block_rows, tile_count + 2, 128)
        window_sums = jnp.zeros((block_rows, tile_count, 128), jnp.float32)
        for k in range(3):
            window_sums = window_sums + jnp.einsum('rtc,tcd->rtd', extended[:, k:k + tile_count], band_weights[:, k], precision=lax.Precision.HIGHEST)
        background = window_sums.reshape(block_rows, BINS) / divisor
        processed = (intensity - background).astype(jnp.bfloat16)
        score_tile = jnp.dot(processed, theory.T, preferred_element_type=jnp.float32)
        return zscores(score_tile, cand_ids)
    cand_scores = lax.map(one_block, (spectra.reshape(-1, block_rows, BINS), cand.reshape(-1, block_rows, K))).reshape(NSPEC, K)
    totals = jax.ops.segment_sum(jax.nn.softplus(cand_scores).reshape(-1), cand.reshape(-1), num_segments=PEPTIDES)
    peptide_score = totals / LOAD
    return (cand_scores, peptide_score)
```

```python
import jax
import jax.numpy as jnp
from jax import lax
from jax.sharding import PartitionSpec as P

HALF = 75
REGION = 512


def halo(block, axis, width):
    count = lax.axis_size(axis)
    forward = [(i, i + 1) for i in range(count - 1)]
    backward = [(target, source) for source, target in forward]
    low = lax.ppermute(block[:, -width:], axis, forward)
    high = lax.ppermute(block[:, :width], axis, backward)
    return jnp.concatenate([low, block, high], axis=1)


def make_band(widths):
    block_iota = lax.broadcasted_iota(jnp.int32, (3, 128, 128), 0)
    input_iota = lax.broadcasted_iota(jnp.int32, (3, 128, 128), 1)
    output_iota = lax.broadcasted_iota(jnp.int32, (3, 128, 128), 2)
    offset = 128 * (block_iota - 1) + input_iota - output_iota
    return jnp.abs(offset)[None] <= widths[:, None, None, None]


def copies_to_all(value, axis):
    count = lax.axis_size(axis)
    spread = jnp.broadcast_to(value[None], (count,) + value.shape)
    return lax.all_to_all(spread, axis, 0, 0, tiled=True)


def on_device(spectra, theory, cand, half):
    row_count, bin_count = spectra.shape
    spec_count = lax.axis_size("spec")
    bucket_count = lax.axis_size("bucket")
    per_bucket = theory.shape[0]
    peptides_all = per_bucket * bucket_count
    position = lax.axis_index("spec")

    gathered = copies_to_all(theory, "bucket").reshape(peptides_all, bin_count)

    extended = halo(spectra, "spec", 128)
    bin_widths = jnp.repeat(half, REGION)
    tile_count = bin_count // 128
    tile_view = extended.reshape(row_count, tile_count + 2, 128)
    band_weights = make_band(jnp.repeat(half, REGION // 128)).astype(jnp.bfloat16)
    window_sums = jnp.zeros((row_count, tile_count, 128), jnp.float32)
    for k in range(3):
        window_sums = window_sums + jnp.einsum(
            "rtc,tcd->rtd",
            tile_view[:, k : k + tile_count],
            band_weights[:, k],
            preferred_element_type=jnp.float32,
        )
    window_sums = window_sums.reshape(row_count, bin_count)
    divisor = (2 * bin_widths + 1).astype(jnp.float32)
    processed = (spectra.astype(jnp.float32) - window_sums / divisor).astype(jnp.bfloat16)

    partial = lax.dot_general(
        processed, gathered, (((1,), (1,)), ((), ())), preferred_element_type=jnp.float32
    )
    partial = partial - jnp.mean(partial, axis=1, keepdims=True)

    own = row_count // spec_count
    parts = lax.all_to_all(
        partial.astype(jnp.bfloat16).reshape(spec_count, own, peptides_all), "spec", 0, 0, tiled=True
    )
    scores = jnp.sum(parts.astype(jnp.float32), axis=0)
    centred = scores - jnp.mean(scores, axis=1, keepdims=True)
    spread = jnp.mean(jnp.square(centred), axis=1, keepdims=True)
    own_cand = lax.dynamic_slice_in_dim(cand, position * own, own, 0)
    ids = lax.broadcasted_iota(jnp.int32, (1, 1, peptides_all), 2)
    picked = jnp.sum(jnp.where(own_cand[:, :, None] == ids, centred[:, None, :], 0.0), axis=2)
    own_scores = picked * lax.rsqrt(spread + 1e-06)

    cand_scores = copies_to_all(own_scores, "spec").reshape(row_count, cand.shape[1])

    share = peptides_all // spec_count
    kept = position * share + lax.broadcasted_iota(jnp.int32, (share, 1, 1), 0)
    soft = jax.nn.softplus(cand_scores)
    evidence = jnp.sum(jnp.where(cand[None] == kept, soft[None], 0.0), axis=1)
    evidence = lax.all_to_all(
        evidence.reshape(bucket_count, share // bucket_count, cand.shape[1]), "bucket", 0, 0, tiled=True
    )
    mean_load = cand.shape[1] * row_count / per_bucket
    peptide_score = jnp.sum(evidence, axis=(0, 2)) / mean_load
    return (cand_scores, peptide_score)


def solution(mesh):
    return jax.shard_map(
        on_device,
        mesh=mesh,
        in_specs=(P("bucket", "spec"), P("bucket", "spec"), P("bucket", None), P("spec")),
        out_specs=(P("bucket", None), P(("spec", "bucket"))),
        check_vma=False,
    )
```

```python
import jax
import jax.numpy as jnp
from jax import lax
from jax.experimental import pallas as pl
from jax.experimental.pallas import tpu as pltpu
from jax.sharding import PartitionSpec as P

REGION = 512
SIDE = 128
TILE = 256

VMEM = pl.BlockSpec(memory_space=pltpu.VMEM)
SMEM = pl.BlockSpec(memory_space=pltpu.SMEM)


def params():
    return pltpu.CompilerParams(vmem_limit_bytes=16 * 1024 * 1024)


def window_kernel(half_ref, spectra_ref, low_ref, high_ref, out_ref, wide_ref):
    bins = spectra_ref.shape[1]
    wide_ref[:, :SIDE] = low_ref[...]
    wide_ref[:, SIDE : SIDE + bins] = spectra_ref[...]
    wide_ref[:, SIDE + bins :] = high_ref[...]
    taken = TILE + 2 * SIDE
    source = lax.broadcasted_iota(jnp.int32, (taken, TILE), 0) - SIDE
    target = lax.broadcasted_iota(jnp.int32, (taken, TILE), 1)
    distance = jnp.abs(source - target)
    for region in range(bins // REGION):
        width = half_ref[region]
        band = jnp.where(distance <= width, 1.0, 0.0).astype(jnp.bfloat16)
        divisor = (2 * width + 1).astype(jnp.float32)
        for tile in range(REGION // TILE):
            at = region * REGION + tile * TILE
            sums = jnp.dot(wide_ref[:, at : at + taken], band, preferred_element_type=jnp.float32)
            middle = wide_ref[:, at + SIDE : at + SIDE + TILE].astype(jnp.float32)
            out_ref[:, at : at + TILE] = (middle - sums / divisor).astype(jnp.bfloat16)


def windowed(half, spectra, low, high):
    rows, bins = spectra.shape
    return pl.pallas_call(
        window_kernel,
        out_shape=jax.ShapeDtypeStruct((rows, bins), jnp.bfloat16),
        in_specs=[SMEM, VMEM, VMEM, VMEM],
        out_specs=VMEM,
        scratch_shapes=[pltpu.VMEM((rows, bins + 2 * SIDE), jnp.bfloat16)],
        compiler_params=params(),
        cost_estimate=pl.CostEstimate(flops=2 * rows * bins * 512, bytes_accessed=4 * rows * bins, transcendentals=0),
    )(half, spectra, low, high)


def score_kernel(processed_ref, theory_ref, out_ref):
    scores = lax.dot_general(
        processed_ref[...],
        theory_ref[...],
        (((1,), (1,)), ((), ())),
        preferred_element_type=jnp.float32,
    )
    scores = scores - jnp.mean(scores, axis=1, keepdims=True)
    out_ref[...] = scores.astype(jnp.bfloat16)


def scored(processed, gathered):
    rows, bins = processed.shape
    peptides = gathered.shape[0]
    return pl.pallas_call(
        score_kernel,
        out_shape=jax.ShapeDtypeStruct((rows, peptides), jnp.bfloat16),
        in_specs=[VMEM, VMEM],
        out_specs=VMEM,
        compiler_params=params(),
        cost_estimate=pl.CostEstimate(
            flops=2 * rows * bins * peptides, bytes_accessed=2 * (rows + peptides) * bins, transcendentals=0
        ),
    )(processed, gathered)


def pick_kernel(position_ref, parts_ref, cand_ref, out_ref):
    count, own, peptides = parts_ref.shape
    lanes = cand_ref.shape[1]
    scores = jnp.sum(parts_ref[...].astype(jnp.float32), axis=0)
    centred = scores - jnp.mean(scores, axis=1, keepdims=True)
    spread = jnp.mean(jnp.square(centred), axis=1, keepdims=True)
    first = pl.multiple_of(position_ref[0] * own, own)
    ids = cand_ref[pl.ds(first, own), :]
    picked = jnp.zeros((own, lanes), jnp.float32)
    for block in range(peptides // lanes):
        part = centred[:, block * lanes : (block + 1) * lanes]
        value = jnp.take_along_axis(part, ids & (lanes - 1), axis=1)
        picked = jnp.where(ids // lanes == block, value, picked)
    result = picked * lax.rsqrt(spread + 1e-06)
    out_ref[...] = jnp.broadcast_to(result[None], out_ref.shape)


def picked_copies(position, parts, cand):
    count, own, peptides = parts.shape
    return pl.pallas_call(
        pick_kernel,
        out_shape=jax.ShapeDtypeStruct((count, own, cand.shape[1]), jnp.float32),
        in_specs=[SMEM, VMEM, VMEM],
        out_specs=VMEM,
        compiler_params=params(),
    )(position, parts, cand)


def evidence_kernel(position_ref, value_ref, cand_ref, out_ref):
    share = out_ref.shape[0]
    rows, lanes = value_ref.shape
    soft = jax.nn.softplus(value_ref[...])
    ids = cand_ref[...] - position_ref[0] * share
    for k in range(share):
        kept = jnp.where(ids == k, soft, 0.0)
        out_ref[k : k + 1, :] = jnp.sum(kept, axis=0, keepdims=True)


def evidence_of(position, values, cand, share):
    return pl.pallas_call(
        evidence_kernel,
        out_shape=jax.ShapeDtypeStruct((share, cand.shape[1]), jnp.float32),
        in_specs=[SMEM, VMEM, VMEM],
        out_specs=VMEM,
        compiler_params=params(),
    )(position, values, cand)


def on_device(spectra, theory, cand, half):
    row_count, bin_count = spectra.shape
    spec_count = lax.axis_size("spec")
    bucket_count = lax.axis_size("bucket")
    per_bucket = theory.shape[0]
    peptides_all = per_bucket * bucket_count
    position = lax.axis_index("spec").astype(jnp.int32).reshape(1)

    copies = jnp.broadcast_to(theory[None], (bucket_count,) + theory.shape)
    copies, observed = lax.optimization_barrier((copies, spectra))
    gathered = lax.all_to_all(copies, "bucket", 0, 0, tiled=True)

    forward = [(i, i + 1) for i in range(spec_count - 1)]
    backward = [(target, source) for source, target in forward]
    low = lax.ppermute(observed[:, -SIDE:], "spec", forward)
    high = lax.ppermute(observed[:, :SIDE], "spec", backward)
    processed = windowed(half, spectra, low, high)

    partial = scored(processed, gathered.reshape(peptides_all, bin_count))

    own = row_count // spec_count
    parts = lax.all_to_all(partial.reshape(spec_count, own, peptides_all), "spec", 0, 0, tiled=True)
    copies = picked_copies(position, parts, cand)
    cand_scores = lax.all_to_all(copies, "spec", 0, 0, tiled=True).reshape(row_count, cand.shape[1])

    share = peptides_all // spec_count
    evidence = evidence_of(position, cand_scores, cand, share)
    evidence = lax.all_to_all(
        evidence.reshape(bucket_count, share // bucket_count, cand.shape[1]), "bucket", 0, 0, tiled=True
    )
    mean_load = cand.shape[1] * row_count / per_bucket
    peptide_score = jnp.sum(evidence, axis=(0, 2)) / mean_load
    return (cand_scores, peptide_score)


def solution(mesh):
    return jax.shard_map(
        on_device,
        mesh=mesh,
        in_specs=(P("bucket", "spec"), P("bucket", "spec"), P("bucket", None), P("spec")),
        out_specs=(P("bucket", None), P(("spec", "bucket"))),
        check_vma=False,
    )
```

```python
import functools

import jax
import jax.numpy as jnp
from jax import lax
from jax.experimental import pallas as pl
from jax.experimental.pallas import tpu as pltpu
from jax.sharding import PartitionSpec as P

REGION = 512
SIDE = 128
TILE = 256

VMEM = pl.BlockSpec(memory_space=pltpu.VMEM)
SMEM = pl.BlockSpec(memory_space=pltpu.SMEM)


def params():
    return pltpu.CompilerParams(vmem_limit_bytes=16 * 1024 * 1024)


def window_kernel(half_ref, spectra_ref, low_ref, high_ref, out_ref, wide_ref):
    bins = spectra_ref.shape[1]
    wide_ref[:, :SIDE] = low_ref[...]
    wide_ref[:, SIDE : SIDE + bins] = spectra_ref[...]
    wide_ref[:, SIDE + bins :] = high_ref[...]
    taken = TILE + 2 * SIDE
    source = lax.broadcasted_iota(jnp.int32, (taken, TILE), 0) - SIDE
    target = lax.broadcasted_iota(jnp.int32, (taken, TILE), 1)
    distance = jnp.abs(source - target)
    for region in range(bins // REGION):
        width = half_ref[region]
        band = jnp.where(distance <= width, 1.0, 0.0).astype(jnp.bfloat16)
        divisor = (2 * width + 1).astype(jnp.float32)
        for tile in range(REGION // TILE):
            at = region * REGION + tile * TILE
            sums = jnp.dot(wide_ref[:, at : at + taken], band, preferred_element_type=jnp.float32)
            middle = wide_ref[:, at + SIDE : at + SIDE + TILE].astype(jnp.float32)
            out_ref[:, at : at + TILE] = (middle - sums / divisor).astype(jnp.bfloat16)


def windowed(half, spectra, low, high):
    rows, bins = spectra.shape
    return pl.pallas_call(
        window_kernel,
        out_shape=jax.ShapeDtypeStruct((rows, bins), jnp.bfloat16),
        in_specs=[SMEM, VMEM, VMEM, VMEM],
        out_specs=VMEM,
        scratch_shapes=[pltpu.VMEM((rows, bins + 2 * SIDE), jnp.bfloat16)],
        compiler_params=params(),
        cost_estimate=pl.CostEstimate(flops=2 * rows * bins * 512, bytes_accessed=4 * rows * bins, transcendentals=0),
    )(half, spectra, low, high)


def score_kernel(core_ref, processed_ref, *refs):
    pieces, keep_ref, send_ref = refs[:-2], refs[-2], refs[-1]
    blocks, own, peptides = keep_ref.shape
    theory = jnp.concatenate([piece[...] for piece in pieces], axis=0)
    scores = lax.dot_general(
        processed_ref[...], theory, (((1,), (1,)), ((), ())), preferred_element_type=jnp.float32
    )
    scores = scores - jnp.mean(scores, axis=1, keepdims=True)
    halves = scores.reshape(blocks, 2, own, peptides)
    even, odd = halves[:, 0], halves[:, 1]
    first = core_ref[0] == 0
    keep_ref[...] = jnp.where(first, even, odd)
    send_ref[...] = jnp.where(first, odd, even)


def scored(core, processed, pieces, own):
    rows, bins = processed.shape
    peptides = sum(piece.shape[0] for piece in pieces)
    half_rows = jax.ShapeDtypeStruct((rows // own // 2, own, peptides), jnp.float32)
    return pl.pallas_call(
        score_kernel,
        out_shape=(half_rows, half_rows),
        in_specs=[SMEM, VMEM] + [VMEM] * len(pieces),
        out_specs=(VMEM, VMEM),
        compiler_params=params(),
        cost_estimate=pl.CostEstimate(
            flops=2 * rows * bins * peptides, bytes_accessed=2 * (rows + peptides) * bins, transcendentals=0
        ),
    )(core, processed, *pieces)


def pick_kernel(where_ref, parts_ref, cand_ref, out_ref):
    count, own, peptides = parts_ref.shape
    lanes = cand_ref.shape[1]
    per_bucket = lanes // 2
    rounds = peptides // lanes
    scores = jnp.sum(parts_ref[...].astype(jnp.float32), axis=0)
    centred = scores - jnp.mean(scores, axis=1, keepdims=True)
    spread = jnp.mean(jnp.square(centred), axis=1, keepdims=True)
    first = pl.multiple_of(where_ref[0] * own, own)
    ids = cand_ref[pl.ds(first, own), :]
    bucket = where_ref[1]
    block_of = (ids // lanes - bucket // 2) & (rounds - 1)
    lane_of = (ids & (lanes - 1)) ^ ((bucket & 1) * per_bucket)
    picked = jnp.zeros((own, lanes), jnp.float32)
    for block in range(rounds):
        part = centred[:, block * lanes : (block + 1) * lanes]
        value = jnp.take_along_axis(part, lane_of, axis=1)
        picked = jnp.where(block_of == block, value, picked)
    result = (picked * lax.rsqrt(spread + 1e-06)).astype(out_ref.dtype)
    out_ref[...] = jnp.broadcast_to(result[None], out_ref.shape)


def picked_copies(where, parts, cand, count):
    own = parts.shape[1]
    return pl.pallas_call(
        pick_kernel,
        out_shape=jax.ShapeDtypeStruct((count, own, cand.shape[1]), jnp.bfloat16),
        in_specs=[SMEM, VMEM, VMEM],
        out_specs=VMEM,
        compiler_params=params(),
    )(where, parts, cand)


def evidence_kernel(load, where_ref, value_ref, cand_ref, wide_ref, out_ref):
    share = out_ref.shape[0]
    rows, lanes = cand_ref.shape
    values = value_ref[...].astype(jnp.float32).reshape(rows, lanes)
    wide_ref[...] = values
    soft = jax.nn.softplus(values)
    ids = cand_ref[...] - where_ref[0] * share
    for k in range(share):
        kept = jnp.where(ids == k, soft, 0.0)
        out_ref[k : k + 1, :] = jnp.sum(kept, axis=0, keepdims=True) / load


def evidence_of(where, values, cand, share, load):
    return pl.pallas_call(
        functools.partial(evidence_kernel, load),
        out_shape=(
            jax.ShapeDtypeStruct(cand.shape, jnp.float32),
            jax.ShapeDtypeStruct((share, cand.shape[1]), jnp.float32),
        ),
        in_specs=[SMEM, VMEM, VMEM],
        out_specs=(VMEM, VMEM),
        compiler_params=params(),
    )(where, values, cand)


def from_all_buckets(shard):
    count = lax.axis_size("bucket")

    def along_y(value, step):
        return lax.ppermute(value, "bucket", [(b, (b - 2 * step) % count) for b in range(count)])

    def along_x(value):
        return lax.ppermute(value, "bucket", [(b, b ^ 1) for b in range(count)])

    beside = along_x(shard)
    above, below, across = along_y(shard, 1), along_y(shard, 3), along_y(shard, 2)
    across_beside = along_y(beside, 2)
    above_beside, below_beside = along_x(above), along_x(below)
    return [shard, beside, above, above_beside, across, across_beside, below, below_beside]


def on_device(spectra, theory, cand, half):
    row_count, bin_count = spectra.shape
    spec_count = lax.axis_size("spec")
    bucket_count = lax.axis_size("bucket")
    per_bucket = theory.shape[0]
    peptides_all = per_bucket * bucket_count
    spec = lax.axis_index("spec").astype(jnp.int32)
    bucket = lax.axis_index("bucket").astype(jnp.int32)
    where = jnp.stack([spec, bucket])
    core = (spec % 2).reshape(1)

    pieces = from_all_buckets(theory)

    forward = [(i, i + 1) for i in range(spec_count - 1)]
    backward = [(target, source) for source, target in forward]
    low = lax.ppermute(spectra[:, -SIDE:], "spec", forward)
    high = lax.ppermute(spectra[:, :SIDE], "spec", backward)
    processed = windowed(half, spectra, low, high)

    own = row_count // spec_count
    keep, send = scored(core, processed, pieces, own)
    got = lax.ppermute(send, "spec", [(i, i ^ 1) for i in range(spec_count)])
    chip = (keep + got).astype(jnp.bfloat16)
    groups = [list(range(c, spec_count, 2)) for c in range(2)]
    parts = lax.all_to_all(chip, "spec", 0, 0, axis_index_groups=groups, tiled=True)
    copies = picked_copies(where, parts, cand, spec_count)
    values = lax.all_to_all(copies, "spec", 0, 0, tiled=True)

    share = peptides_all // spec_count
    mean_load = cand.shape[1] * row_count / per_bucket
    cand_scores, evidence = evidence_of(where, values, cand, share, mean_load)
    evidence = lax.all_to_all(
        evidence.reshape(bucket_count, share // bucket_count, cand.shape[1]), "bucket", 0, 0, tiled=True
    )
    return (cand_scores, jnp.sum(evidence, axis=(0, 2)))


def solution(mesh):
    return jax.shard_map(
        on_device,
        mesh=mesh,
        in_specs=(P("bucket", "spec"), P("bucket", "spec"), P("bucket", None), P("spec")),
        out_specs=(P("bucket", None), P(("spec", "bucket"))),
        check_vma=False,
    )
```

```python
import functools

import jax
import jax.numpy as jnp
from jax import lax
from jax.experimental import pallas as pl
from jax.experimental.pallas import tpu as pltpu
from jax.sharding import PartitionSpec as P

REGION = 512
SIDE = 128
TILE = 256

VMEM = pl.BlockSpec(memory_space=pltpu.VMEM)
SMEM = pl.BlockSpec(memory_space=pltpu.SMEM)


def params():
    return pltpu.CompilerParams(vmem_limit_bytes=16 * 1024 * 1024)


def window_kernel(half_ref, spectra_ref, low_ref, high_ref, out_ref, wide_ref):
    bins = spectra_ref.shape[1]
    wide_ref[:, :SIDE] = low_ref[...]
    wide_ref[:, SIDE : SIDE + bins] = spectra_ref[...]
    wide_ref[:, SIDE + bins :] = high_ref[...]
    taken = TILE + 2 * SIDE
    source = lax.broadcasted_iota(jnp.int32, (taken, TILE), 0) - SIDE
    target = lax.broadcasted_iota(jnp.int32, (taken, TILE), 1)
    distance = jnp.abs(source - target)
    for region in range(bins // REGION):
        width = half_ref[region]
        band = jnp.where(distance <= width, 1.0, 0.0).astype(jnp.bfloat16)
        divisor = (2 * width + 1).astype(jnp.float32)
        for tile in range(REGION // TILE):
            at = region * REGION + tile * TILE
            sums = jnp.dot(wide_ref[:, at : at + taken], band, preferred_element_type=jnp.float32)
            middle = wide_ref[:, at + SIDE : at + SIDE + TILE].astype(jnp.float32)
            out_ref[:, at : at + TILE] = (middle - sums / divisor).astype(jnp.bfloat16)


def windowed(half, spectra, low, high):
    rows, bins = spectra.shape
    return pl.pallas_call(
        window_kernel,
        out_shape=jax.ShapeDtypeStruct((rows, bins), jnp.bfloat16),
        in_specs=[SMEM, VMEM, VMEM, VMEM],
        out_specs=VMEM,
        scratch_shapes=[pltpu.VMEM((rows, bins + 2 * SIDE), jnp.bfloat16)],
        compiler_params=params(),
        cost_estimate=pl.CostEstimate(flops=2 * rows * bins * 512, bytes_accessed=4 * rows * bins, transcendentals=0),
    )(half, spectra, low, high)


def score_kernel(core_ref, processed_ref, theory_ref, keep_ref, send_ref):
    blocks, own, peptides = keep_ref.shape
    scores = lax.dot_general(
        processed_ref[...], theory_ref[...], (((1,), (1,)), ((), ())), preferred_element_type=jnp.float32
    )
    scores = scores - jnp.mean(scores, axis=1, keepdims=True)
    halves = scores.reshape(blocks, 2, own, peptides)
    even, odd = halves[:, 0], halves[:, 1]
    first = core_ref[0] == 0
    keep_ref[...] = jnp.where(first, even, odd)
    send_ref[...] = jnp.where(first, odd, even)


def scored(core, processed, gathered, own):
    rows, bins = processed.shape
    peptides = gathered.shape[0]
    half_rows = jax.ShapeDtypeStruct((rows // own // 2, own, peptides), jnp.float32)
    return pl.pallas_call(
        score_kernel,
        out_shape=(half_rows, half_rows),
        in_specs=[SMEM, VMEM, VMEM],
        out_specs=(VMEM, VMEM),
        compiler_params=params(),
        cost_estimate=pl.CostEstimate(
            flops=2 * rows * bins * peptides, bytes_accessed=2 * (rows + peptides) * bins, transcendentals=0
        ),
    )(core, processed, gathered)


def pick_kernel(where_ref, parts_ref, cand_ref, out_ref):
    count, own, peptides = parts_ref.shape
    lanes = cand_ref.shape[1]
    scores = jnp.sum(parts_ref[...].astype(jnp.float32), axis=0)
    centred = scores - jnp.mean(scores, axis=1, keepdims=True)
    spread = jnp.mean(jnp.square(centred), axis=1, keepdims=True)
    first = pl.multiple_of(where_ref[0] * own, own)
    ids = cand_ref[pl.ds(first, own), :]
    block_of = ids // lanes
    lane_of = ids & (lanes - 1)
    picked = jnp.zeros((own, lanes), jnp.float32)
    for block in range(peptides // lanes):
        part = centred[:, block * lanes : (block + 1) * lanes]
        value = jnp.take_along_axis(part, lane_of, axis=1)
        picked = jnp.where(block_of == block, value, picked)
    result = (picked * lax.rsqrt(spread + 1e-06)).astype(out_ref.dtype)
    out_ref[...] = jnp.broadcast_to(result[None], out_ref.shape)


def picked_copies(where, parts, cand, count):
    own = parts.shape[1]
    return pl.pallas_call(
        pick_kernel,
        out_shape=jax.ShapeDtypeStruct((count, own, cand.shape[1]), jnp.bfloat16),
        in_specs=[SMEM, VMEM, VMEM],
        out_specs=VMEM,
        compiler_params=params(),
    )(where, parts, cand)


def evidence_kernel(load, where_ref, value_ref, cand_ref, out_ref):
    share = out_ref.shape[0]
    rows, lanes = cand_ref.shape
    values = value_ref[...].astype(jnp.float32).reshape(rows, lanes)
    soft = jax.nn.softplus(values)
    ids = cand_ref[...] - where_ref[0] * share
    for k in range(share):
        kept = jnp.where(ids == k, soft, 0.0)
        out_ref[k : k + 1, :] = jnp.sum(kept, axis=0, keepdims=True) / load


def evidence_of(where, values, cand, share, load):
    return pl.pallas_call(
        functools.partial(evidence_kernel, load),
        out_shape=jax.ShapeDtypeStruct((share, cand.shape[1]), jnp.float32),
        in_specs=[SMEM, VMEM, VMEM],
        out_specs=VMEM,
        compiler_params=params(),
    )(where, values, cand)


def on_device(spectra, theory, cand, half):
    row_count, bin_count = spectra.shape
    spec_count = lax.axis_size("spec")
    bucket_count = lax.axis_size("bucket")
    per_bucket = theory.shape[0]
    peptides_all = per_bucket * bucket_count
    spec = lax.axis_index("spec").astype(jnp.int32)
    where = spec.reshape(1)
    core = (spec % 2).reshape(1)

    copies = jnp.broadcast_to(theory[None], (bucket_count,) + theory.shape)
    copies, observed = lax.optimization_barrier((copies, spectra))
    gathered = lax.all_to_all(copies, "bucket", 0, 0, tiled=True).reshape(peptides_all, bin_count)

    forward = [(i, i + 1) for i in range(spec_count - 1)]
    backward = [(target, source) for source, target in forward]
    low = lax.ppermute(observed[:, -SIDE:], "spec", forward)
    high = lax.ppermute(observed[:, :SIDE], "spec", backward)
    processed = windowed(half, spectra, low, high)

    own = row_count // spec_count
    keep, send = scored(core, processed, gathered, own)
    got = lax.ppermute(send, "spec", [(i, i ^ 1) for i in range(spec_count)])
    chip = (keep + got).astype(jnp.bfloat16)
    groups = [list(range(c, spec_count, 2)) for c in range(2)]
    parts = lax.all_to_all(chip, "spec", 0, 0, axis_index_groups=groups, tiled=True)
    copies = picked_copies(where, parts, cand, spec_count)
    values = lax.all_to_all(copies, "spec", 0, 0, tiled=True)

    share = peptides_all // spec_count
    mean_load = cand.shape[1] * row_count / per_bucket
    evidence = evidence_of(where, values, cand, share, mean_load)
    cand_scores = values.astype(jnp.float32).reshape(row_count, cand.shape[1])
    evidence = lax.all_to_all(
        evidence.reshape(bucket_count, share // bucket_count, cand.shape[1]), "bucket", 0, 0, tiled=True
    )
    return (cand_scores, jnp.sum(evidence, axis=(0, 2)))


def solution(mesh):
    return jax.shard_map(
        on_device,
        mesh=mesh,
        in_specs=(P("bucket", "spec"), P("bucket", "spec"), P("bucket", None), P("spec")),
        out_specs=(P("bucket", None), P(("spec", "bucket"))),
        check_vma=False,
    )
```

```python
import functools

import jax
import jax.numpy as jnp
from jax import lax
from jax.experimental import pallas as pl
from jax.experimental.pallas import tpu as pltpu
from jax.sharding import PartitionSpec as P

REGION = 512
SIDE = 128
TILE = 256

VMEM = pl.BlockSpec(memory_space=pltpu.VMEM)
SMEM = pl.BlockSpec(memory_space=pltpu.SMEM)


def params():
    return pltpu.CompilerParams(vmem_limit_bytes=16 * 1024 * 1024)


def window_kernel(half_ref, spectra_ref, low_ref, high_ref, out_ref, wide_ref):
    bins = spectra_ref.shape[1]
    wide_ref[:, :SIDE] = low_ref[...]
    wide_ref[:, SIDE : SIDE + bins] = spectra_ref[...]
    wide_ref[:, SIDE + bins :] = high_ref[...]
    taken = TILE + 2 * SIDE
    source = lax.broadcasted_iota(jnp.int32, (taken, TILE), 0) - SIDE
    target = lax.broadcasted_iota(jnp.int32, (taken, TILE), 1)
    distance = jnp.abs(source - target)
    for region in range(bins // REGION):
        width = half_ref[region]
        band = jnp.where(distance <= width, 1.0, 0.0).astype(jnp.bfloat16)
        divisor = (2 * width + 1).astype(jnp.float32)
        for tile in range(REGION // TILE):
            at = region * REGION + tile * TILE
            sums = jnp.dot(wide_ref[:, at : at + taken], band, preferred_element_type=jnp.float32)
            middle = wide_ref[:, at + SIDE : at + SIDE + TILE].astype(jnp.float32)
            out_ref[:, at : at + TILE] = (middle - sums / divisor).astype(jnp.bfloat16)


def windowed(half, spectra, low, high):
    rows, bins = spectra.shape
    return pl.pallas_call(
        window_kernel,
        out_shape=jax.ShapeDtypeStruct((rows, bins), jnp.bfloat16),
        in_specs=[SMEM, VMEM, VMEM, VMEM],
        out_specs=VMEM,
        scratch_shapes=[pltpu.VMEM((rows, bins + 2 * SIDE), jnp.bfloat16)],
        compiler_params=params(),
        cost_estimate=pl.CostEstimate(flops=2 * rows * bins * 512, bytes_accessed=4 * rows * bins, transcendentals=0),
    )(half, spectra, low, high)


def score_kernel(core_ref, processed_ref, *refs):
    pieces, keep_ref, send_ref = refs[:-2], refs[-2], refs[-1]
    blocks, own, peptides = keep_ref.shape
    theory = jnp.concatenate([piece[...] for piece in pieces], axis=0)
    scores = lax.dot_general(
        processed_ref[...], theory, (((1,), (1,)), ((), ())), preferred_element_type=jnp.float32
    )
    scores = scores - jnp.mean(scores, axis=1, keepdims=True)
    halves = scores.reshape(blocks, 2, own, peptides)
    even, odd = halves[:, 0], halves[:, 1]
    first = core_ref[0] == 0
    keep_ref[...] = jnp.where(first, even, odd)
    send_ref[...] = jnp.where(first, odd, even)


def scored(core, processed, pieces, own):
    rows, bins = processed.shape
    peptides = sum(piece.shape[0] for piece in pieces)
    half_rows = jax.ShapeDtypeStruct((rows // own // 2, own, peptides), jnp.float32)
    return pl.pallas_call(
        score_kernel,
        out_shape=(half_rows, half_rows),
        in_specs=[SMEM, VMEM] + [VMEM] * len(pieces),
        out_specs=(VMEM, VMEM),
        compiler_params=params(),
        cost_estimate=pl.CostEstimate(
            flops=2 * rows * bins * peptides, bytes_accessed=2 * (rows + peptides) * bins, transcendentals=0
        ),
    )(core, processed, *pieces)


def pick_kernel(spec_ref, bucket_ref, parts_ref, cand_ref, out_ref):
    count, own, peptides = parts_ref.shape
    lanes = cand_ref.shape[1]
    per_bucket = lanes // 2
    rounds = peptides // lanes
    scores = jnp.sum(parts_ref[...].astype(jnp.float32), axis=0)
    centred = scores - jnp.mean(scores, axis=1, keepdims=True)
    spread = jnp.mean(jnp.square(centred), axis=1, keepdims=True)
    first = pl.multiple_of(spec_ref[0] * own, own)
    ids = cand_ref[pl.ds(first, own), :]
    bucket = bucket_ref[0]
    block_of = (ids // lanes - bucket // 2) & (rounds - 1)
    lane_of = (ids & (lanes - 1)) ^ ((bucket & 1) * per_bucket)
    picked = jnp.zeros((own, lanes), jnp.float32)
    for block in range(rounds):
        part = centred[:, block * lanes : (block + 1) * lanes]
        value = jnp.take_along_axis(part, lane_of, axis=1)
        picked = jnp.where(block_of == block, value, picked)
    result = (picked * lax.rsqrt(spread + 1e-06)).astype(out_ref.dtype)
    out_ref[...] = jnp.broadcast_to(result[None], out_ref.shape)


def picked_copies(where, parts, cand, count):
    own = parts.shape[1]
    return pl.pallas_call(
        pick_kernel,
        out_shape=jax.ShapeDtypeStruct((count, own, cand.shape[1]), jnp.bfloat16),
        in_specs=[SMEM, SMEM, VMEM, VMEM],
        out_specs=VMEM,
        compiler_params=params(),
    )(*where, parts, cand)


def evidence_kernel(load, spec_ref, value_ref, cand_ref, out_ref):
    share = out_ref.shape[0]
    rows, lanes = cand_ref.shape
    values = value_ref[...].astype(jnp.float32).reshape(rows, lanes)
    soft = jax.nn.softplus(values)
    ids = cand_ref[...] - spec_ref[0] * share
    for k in range(share):
        kept = jnp.where(ids == k, soft, 0.0)
        out_ref[k : k + 1, :] = jnp.sum(kept, axis=0, keepdims=True) / load


def evidence_of(where, values, cand, share, load):
    return pl.pallas_call(
        functools.partial(evidence_kernel, load),
        out_shape=jax.ShapeDtypeStruct((share, cand.shape[1]), jnp.float32),
        in_specs=[SMEM, VMEM, VMEM],
        out_specs=VMEM,
        compiler_params=params(),
    )(where[0], values, cand)


def last_kernel(value_ref, evidence_ref, wide_ref, out_ref):
    wide_ref[...] = value_ref[...].astype(jnp.float32).reshape(wide_ref.shape)
    total = jnp.sum(jnp.sum(evidence_ref[...], axis=0), axis=1, keepdims=True)
    out_ref[...] = jnp.broadcast_to(total, out_ref.shape)


def last_step(values, evidence):
    return pl.pallas_call(
        last_kernel,
        out_shape=(
            jax.ShapeDtypeStruct((values.shape[0] * values.shape[1], values.shape[2]), jnp.float32),
            jax.ShapeDtypeStruct(evidence.shape[1:], jnp.float32),
        ),
        in_specs=[VMEM, VMEM],
        out_specs=(VMEM, VMEM),
        compiler_params=params(),
    )(values, evidence)


def from_all_buckets(shard, beside_work):
    count = lax.axis_size("bucket")

    def along_y(value, step):
        return lax.ppermute(value, "bucket", [(b, (b - 2 * step) % count) for b in range(count)])

    def along_x(value):
        return lax.ppermute(value, "bucket", [(b, b ^ 1) for b in range(count)])

    beside = along_x(shard)
    above, below, across = along_y(shard, 1), along_y(shard, 3), along_y(shard, 2)
    beside, across, processed = lax.optimization_barrier((beside, across, beside_work))
    above_beside, below_beside = along_y(beside, 1), along_y(beside, 3)
    across_beside = along_x(across)
    return processed, [shard, beside, above, above_beside, across, across_beside, below, below_beside]


def on_device(spectra, theory, cand, half):
    row_count, bin_count = spectra.shape
    spec_count = lax.axis_size("spec")
    bucket_count = lax.axis_size("bucket")
    per_bucket = theory.shape[0]
    peptides_all = per_bucket * bucket_count
    spec = lax.axis_index("spec").astype(jnp.int32)
    bucket = lax.axis_index("bucket").astype(jnp.int32)
    where = spec.reshape(1), bucket.reshape(1)
    core = (spec % 2).reshape(1)

    theory, low, high = lax.optimization_barrier((theory, spectra[:, -SIDE:], spectra[:, :SIDE]))

    forward = [(i, i + 1) for i in range(spec_count - 1)]
    backward = [(target, source) for source, target in forward]
    low = lax.ppermute(low, "spec", forward)
    high = lax.ppermute(high, "spec", backward)
    processed = windowed(half, spectra, low, high)
    processed, pieces = from_all_buckets(theory, processed)

    own = row_count // spec_count
    keep, send = scored(core, processed, pieces, own)
    got = lax.ppermute(send, "spec", [(i, i ^ 1) for i in range(spec_count)])
    chip = (keep + got).astype(jnp.bfloat16)
    groups = [list(range(c, spec_count, 2)) for c in range(2)]
    parts = lax.all_to_all(chip, "spec", 0, 0, axis_index_groups=groups, tiled=True)
    copies = picked_copies(where, parts, cand, spec_count)
    values = lax.all_to_all(copies, "spec", 0, 0, tiled=True)

    share = peptides_all // spec_count
    mean_load = cand.shape[1] * row_count / per_bucket
    evidence = evidence_of(where, values, cand, share, mean_load)
    evidence = lax.all_to_all(
        evidence.reshape(bucket_count, share // bucket_count, cand.shape[1]), "bucket", 0, 0, tiled=True
    )
    cand_scores, totals = last_step(values, evidence)
    return (cand_scores, totals[:, 0])


def solution(mesh):
    return jax.shard_map(
        on_device,
        mesh=mesh,
        in_specs=(P("bucket", "spec"), P("bucket", "spec"), P("bucket", None), P("spec")),
        out_specs=(P("bucket", None), P(("spec", "bucket"))),
        check_vma=False,
    )
```

```python
import functools

import jax
import jax.numpy as jnp
from jax import lax
from jax.experimental import pallas as pl
from jax.experimental.pallas import tpu as pltpu
from jax.sharding import PartitionSpec as P

REGION = 512
SIDE = 128
TILE = 256

VMEM = pl.BlockSpec(memory_space=pltpu.VMEM)
SMEM = pl.BlockSpec(memory_space=pltpu.SMEM)


def params():
    return pltpu.CompilerParams(vmem_limit_bytes=16 * 1024 * 1024)


def window_kernel(half_ref, spec_ref, bucket_ref, spectra_ref, low_ref, high_ref, cand_ref, out_ref, near_ref, wide_ref):
    near_ref[...] = cand_ref[...]
    bins = spectra_ref.shape[1]
    wide_ref[:, :SIDE] = low_ref[...]
    wide_ref[:, SIDE : SIDE + bins] = spectra_ref[...]
    wide_ref[:, SIDE + bins :] = high_ref[...]
    taken = TILE + 2 * SIDE
    source = lax.broadcasted_iota(jnp.int32, (taken, TILE), 0) - SIDE
    target = lax.broadcasted_iota(jnp.int32, (taken, TILE), 1)
    distance = jnp.abs(source - target)
    for region in range(bins // REGION):
        width = half_ref[region]
        band = jnp.where(distance <= width, 1.0, 0.0).astype(jnp.bfloat16)
        divisor = (2 * width + 1).astype(jnp.float32)
        for tile in range(REGION // TILE):
            at = region * REGION + tile * TILE
            sums = jnp.dot(wide_ref[:, at : at + taken], band, preferred_element_type=jnp.float32)
            middle = wide_ref[:, at + SIDE : at + SIDE + TILE].astype(jnp.float32)
            out_ref[:, at : at + TILE] = (middle - sums / divisor).astype(jnp.bfloat16)


def windowed(half, where, spectra, low, high, cand):
    rows, bins = spectra.shape
    return pl.pallas_call(
        window_kernel,
        out_shape=(jax.ShapeDtypeStruct((rows, bins), jnp.bfloat16), jax.ShapeDtypeStruct(cand.shape, cand.dtype)),
        in_specs=[SMEM, SMEM, SMEM, VMEM, VMEM, VMEM, VMEM],
        out_specs=(VMEM, VMEM),
        scratch_shapes=[pltpu.VMEM((rows, bins + 2 * SIDE), jnp.bfloat16)],
        compiler_params=params(),
        cost_estimate=pl.CostEstimate(flops=2 * rows * bins * 512, bytes_accessed=4 * rows * bins, transcendentals=0),
    )(half, *where, spectra, low, high, cand)


def score_kernel(core_ref, processed_ref, *refs):
    pieces, keep_ref, send_ref = refs[:-2], refs[-2], refs[-1]
    blocks, own, peptides = keep_ref.shape
    theory = jnp.concatenate([piece[...] for piece in pieces], axis=0)
    scores = lax.dot_general(
        processed_ref[...], theory, (((1,), (1,)), ((), ())), preferred_element_type=jnp.float32
    )
    scores = scores - jnp.mean(scores, axis=1, keepdims=True)
    halves = scores.reshape(blocks, 2, own, peptides)
    even, odd = halves[:, 0], halves[:, 1]
    first = core_ref[0] == 0
    keep_ref[...] = jnp.where(first, even, odd)
    send_ref[...] = jnp.where(first, odd, even)


def scored(core, processed, pieces, own):
    rows, bins = processed.shape
    peptides = sum(piece.shape[0] for piece in pieces)
    half_rows = jax.ShapeDtypeStruct((rows // own // 2, own, peptides), jnp.float32)
    return pl.pallas_call(
        score_kernel,
        out_shape=(half_rows, half_rows),
        in_specs=[SMEM, VMEM] + [VMEM] * len(pieces),
        out_specs=(VMEM, VMEM),
        compiler_params=params(),
        cost_estimate=pl.CostEstimate(
            flops=2 * rows * bins * peptides, bytes_accessed=2 * (rows + peptides) * bins, transcendentals=0
        ),
    )(core, processed, *pieces)


def pick_kernel(spec_ref, bucket_ref, parts_ref, cand_ref, out_ref):
    count, own, peptides = parts_ref.shape
    lanes = cand_ref.shape[1]
    per_bucket = lanes // 2
    rounds = peptides // lanes
    scores = jnp.sum(parts_ref[...].astype(jnp.float32), axis=0)
    centred = scores - jnp.mean(scores, axis=1, keepdims=True)
    spread = jnp.mean(jnp.square(centred), axis=1, keepdims=True)
    first = pl.multiple_of(spec_ref[0] * own, own)
    ids = cand_ref[pl.ds(first, own), :]
    bucket = bucket_ref[0]
    block_of = (ids // lanes - bucket // 2) & (rounds - 1)
    lane_of = (ids & (lanes - 1)) ^ ((bucket & 1) * per_bucket)
    picked = jnp.zeros((own, lanes), jnp.float32)
    for block in range(rounds):
        part = centred[:, block * lanes : (block + 1) * lanes]
        value = jnp.take_along_axis(part, lane_of, axis=1)
        picked = jnp.where(block_of == block, value, picked)
    result = (picked * lax.rsqrt(spread + 1e-06)).astype(out_ref.dtype)
    out_ref[...] = jnp.broadcast_to(result[None], out_ref.shape)


def picked_copies(where, parts, cand, count):
    own = parts.shape[1]
    return pl.pallas_call(
        pick_kernel,
        out_shape=jax.ShapeDtypeStruct((count, own, cand.shape[1]), jnp.bfloat16),
        in_specs=[SMEM, SMEM, VMEM, VMEM],
        out_specs=VMEM,
        compiler_params=params(),
    )(*where, parts, cand)


def evidence_kernel(load, spec_ref, value_ref, cand_ref, out_ref):
    share = out_ref.shape[0]
    rows, lanes = cand_ref.shape
    values = value_ref[...].astype(jnp.float32).reshape(rows, lanes)
    soft = jax.nn.softplus(values)
    ids = cand_ref[...] - spec_ref[0] * share
    for k in range(share):
        kept = jnp.where(ids == k, soft, 0.0)
        out_ref[k : k + 1, :] = jnp.sum(kept, axis=0, keepdims=True) / load


def evidence_of(where, values, cand, share, load):
    return pl.pallas_call(
        functools.partial(evidence_kernel, load),
        out_shape=jax.ShapeDtypeStruct((share, cand.shape[1]), jnp.float32),
        in_specs=[SMEM, VMEM, VMEM],
        out_specs=VMEM,
        compiler_params=params(),
    )(where[0], values, cand)


def last_kernel(value_ref, evidence_ref, wide_ref, out_ref):
    wide_ref[...] = value_ref[...].astype(jnp.float32).reshape(wide_ref.shape)
    total = jnp.sum(jnp.sum(evidence_ref[...], axis=0), axis=1, keepdims=True)
    column = lax.broadcasted_iota(jnp.int32, out_ref.shape, 1)
    row = jnp.zeros(out_ref.shape, jnp.float32)
    for k in range(out_ref.shape[1]):
        row = jnp.where(column == k, total[k : k + 1], row)
    out_ref[...] = row


def last_step(values, evidence):
    return pl.pallas_call(
        last_kernel,
        out_shape=(
            jax.ShapeDtypeStruct((values.shape[0] * values.shape[1], values.shape[2]), jnp.float32),
            jax.ShapeDtypeStruct((1, evidence.shape[1]), jnp.float32),
        ),
        in_specs=[VMEM, VMEM],
        out_specs=(VMEM, VMEM),
        compiler_params=params(),
    )(values, evidence)


def from_all_buckets(shard, low, high):
    count = lax.axis_size("bucket")

    def along_y(value, step):
        return lax.ppermute(value, "bucket", [(b, (b - 2 * step) % count) for b in range(count)])

    def along_x(value):
        return lax.ppermute(value, "bucket", [(b, b ^ 1) for b in range(count)])

    beside = along_x(shard)
    above, below, across = along_y(shard, 1), along_y(shard, 3), along_y(shard, 2)
    beside, across, low, high = lax.optimization_barrier((beside, across, low, high))
    above_beside, below_beside = along_y(beside, 1), along_y(beside, 3)
    across_beside = along_x(across)
    return low, high, [shard, beside, above, above_beside, across, across_beside, below, below_beside]


def on_device(spectra, theory, cand, half):
    row_count, bin_count = spectra.shape
    spec_count = lax.axis_size("spec")
    bucket_count = lax.axis_size("bucket")
    per_bucket = theory.shape[0]
    peptides_all = per_bucket * bucket_count
    spec = lax.axis_index("spec").astype(jnp.int32)
    bucket = lax.axis_index("bucket").astype(jnp.int32)
    where = spec.reshape(1), bucket.reshape(1)
    core = (spec % 2).reshape(1)

    theory, low, high = lax.optimization_barrier((theory, spectra[:, -SIDE:], spectra[:, :SIDE]))

    forward = [(i, i + 1) for i in range(spec_count - 1)]
    backward = [(target, source) for source, target in forward]
    low = lax.ppermute(low, "spec", forward)
    high = lax.ppermute(high, "spec", backward)
    low, high, pieces = from_all_buckets(theory, low, high)
    processed, cand = windowed(half, where, spectra, low, high, cand)

    own = row_count // spec_count
    keep, send = scored(core, processed, pieces, own)
    got = lax.ppermute(send, "spec", [(i, i ^ 1) for i in range(spec_count)])
    chip = (keep + got).astype(jnp.bfloat16)
    groups = [list(range(c, spec_count, 2)) for c in range(2)]
    parts = lax.all_to_all(chip, "spec", 0, 0, axis_index_groups=groups, tiled=True)
    copies = picked_copies(where, parts, cand, spec_count)
    values = lax.all_to_all(copies, "spec", 0, 0, tiled=True)

    share = peptides_all // spec_count
    mean_load = cand.shape[1] * row_count / per_bucket
    evidence = evidence_of(where, values, cand, share, mean_load)
    evidence = lax.all_to_all(
        evidence.reshape(bucket_count, share // bucket_count, cand.shape[1]), "bucket", 0, 0, tiled=True
    )
    cand_scores, totals = last_step(values, evidence)
    return (cand_scores, totals.reshape(-1))


def solution(mesh):
    return jax.shard_map(
        on_device,
        mesh=mesh,
        in_specs=(P("bucket", "spec"), P("bucket", "spec"), P("bucket", None), P("spec")),
        out_specs=(P("bucket", None), P(("spec", "bucket"))),
        check_vma=False,
    )
```

```python
import functools

import jax
import jax.numpy as jnp
from jax import lax
from jax.experimental import pallas as pl
from jax.experimental.pallas import tpu as pltpu
from jax.sharding import PartitionSpec as P

REGION = 512
SIDE = 128
TILE = 256

VMEM = pl.BlockSpec(memory_space=pltpu.VMEM)
SMEM = pl.BlockSpec(memory_space=pltpu.SMEM)


def params():
    return pltpu.CompilerParams(vmem_limit_bytes=16 * 1024 * 1024)


def window_kernel(half_ref, spec_ref, bucket_ref, spectra_ref, inner_ref, outer_ref, cand_ref, out_ref, near_ref, wide_ref):
    near_ref[...] = cand_ref[...]
    bins = spectra_ref.shape[1]
    inner, outer = inner_ref[...], outer_ref[...]
    even_core = spec_ref[0] % 2 == 0
    wide_ref[:, :SIDE] = jnp.where(even_core, outer, inner)
    wide_ref[:, SIDE : SIDE + bins] = spectra_ref[...]
    wide_ref[:, SIDE + bins :] = jnp.where(even_core, inner, outer)
    taken = TILE + 2 * SIDE
    source = lax.broadcasted_iota(jnp.int32, (taken, TILE), 0) - SIDE
    target = lax.broadcasted_iota(jnp.int32, (taken, TILE), 1)
    distance = jnp.abs(source - target)
    for region in range(bins // REGION):
        width = half_ref[region]
        band = jnp.where(distance <= width, 1.0, 0.0).astype(jnp.bfloat16)
        divisor = (2 * width + 1).astype(jnp.float32)
        for tile in range(REGION // TILE):
            at = region * REGION + tile * TILE
            sums = jnp.dot(wide_ref[:, at : at + taken], band, preferred_element_type=jnp.float32)
            middle = wide_ref[:, at + SIDE : at + SIDE + TILE].astype(jnp.float32)
            out_ref[:, at : at + TILE] = (middle - sums / divisor).astype(jnp.bfloat16)


def windowed(half, where, spectra, inner, outer, cand):
    rows, bins = spectra.shape
    return pl.pallas_call(
        window_kernel,
        out_shape=(jax.ShapeDtypeStruct((rows, bins), jnp.bfloat16), jax.ShapeDtypeStruct(cand.shape, cand.dtype)),
        in_specs=[SMEM, SMEM, SMEM, VMEM, VMEM, VMEM, VMEM],
        out_specs=(VMEM, VMEM),
        scratch_shapes=[pltpu.VMEM((rows, bins + 2 * SIDE), jnp.bfloat16)],
        compiler_params=params(),
        cost_estimate=pl.CostEstimate(flops=2 * rows * bins * 512, bytes_accessed=4 * rows * bins, transcendentals=0),
    )(half, *where, spectra, inner, outer, cand)


def score_kernel(core_ref, processed_ref, *refs):
    pieces, keep_ref, send_ref = refs[:-2], refs[-2], refs[-1]
    blocks, own, peptides = keep_ref.shape
    theory = jnp.concatenate([piece[...] for piece in pieces], axis=0)
    scores = lax.dot_general(
        processed_ref[...], theory, (((1,), (1,)), ((), ())), preferred_element_type=jnp.float32
    )
    scores = scores - jnp.mean(scores, axis=1, keepdims=True)
    halves = scores.reshape(blocks, 2, own, peptides)
    even, odd = halves[:, 0], halves[:, 1]
    first = core_ref[0] == 0
    keep_ref[...] = jnp.where(first, even, odd)
    send_ref[...] = jnp.where(first, odd, even)


def scored(core, processed, pieces, own):
    rows, bins = processed.shape
    peptides = sum(piece.shape[0] for piece in pieces)
    half_rows = jax.ShapeDtypeStruct((rows // own // 2, own, peptides), jnp.float32)
    return pl.pallas_call(
        score_kernel,
        out_shape=(half_rows, half_rows),
        in_specs=[SMEM, VMEM] + [VMEM] * len(pieces),
        out_specs=(VMEM, VMEM),
        compiler_params=params(),
        cost_estimate=pl.CostEstimate(
            flops=2 * rows * bins * peptides, bytes_accessed=2 * (rows + peptides) * bins, transcendentals=0
        ),
    )(core, processed, *pieces)


def pick_kernel(spec_ref, bucket_ref, parts_ref, cand_ref, out_ref):
    count, own, peptides = parts_ref.shape
    lanes = cand_ref.shape[1]
    per_bucket = lanes // 2
    rounds = peptides // lanes
    scores = jnp.sum(parts_ref[...].astype(jnp.float32), axis=0)
    centred = scores - jnp.mean(scores, axis=1, keepdims=True)
    spread = jnp.mean(jnp.square(centred), axis=1, keepdims=True)
    first = pl.multiple_of(spec_ref[0] * own, own)
    ids = cand_ref[pl.ds(first, own), :]
    bucket = bucket_ref[0]
    block_of = (ids // lanes - bucket // 2) & (rounds - 1)
    lane_of = (ids & (lanes - 1)) ^ ((bucket & 1) * per_bucket)
    picked = jnp.zeros((own, lanes), jnp.float32)
    for block in range(rounds):
        part = centred[:, block * lanes : (block + 1) * lanes]
        value = jnp.take_along_axis(part, lane_of, axis=1)
        picked = jnp.where(block_of == block, value, picked)
    result = (picked * lax.rsqrt(spread + 1e-06)).astype(out_ref.dtype)
    out_ref[...] = jnp.broadcast_to(result[None], out_ref.shape)


def picked_copies(where, parts, cand, count):
    own = parts.shape[1]
    return pl.pallas_call(
        pick_kernel,
        out_shape=jax.ShapeDtypeStruct((count, own, cand.shape[1]), jnp.bfloat16),
        in_specs=[SMEM, SMEM, VMEM, VMEM],
        out_specs=VMEM,
        compiler_params=params(),
    )(*where, parts, cand)


def evidence_kernel(load, spec_ref, value_ref, cand_ref, out_ref):
    share = out_ref.shape[0]
    rows, lanes = cand_ref.shape
    values = value_ref[...].astype(jnp.float32).reshape(rows, lanes)
    soft = jax.nn.softplus(values)
    ids = cand_ref[...] - spec_ref[0] * share
    for k in range(share):
        kept = jnp.where(ids == k, soft, 0.0)
        out_ref[k : k + 1, :] = jnp.sum(kept, axis=0, keepdims=True) / load


def evidence_of(where, values, cand, share, load):
    return pl.pallas_call(
        functools.partial(evidence_kernel, load),
        out_shape=jax.ShapeDtypeStruct((share, cand.shape[1]), jnp.float32),
        in_specs=[SMEM, VMEM, VMEM],
        out_specs=VMEM,
        compiler_params=params(),
    )(where[0], values, cand)


def last_kernel(value_ref, evidence_ref, wide_ref, out_ref):
    wide_ref[...] = value_ref[...].astype(jnp.float32).reshape(wide_ref.shape)
    total = jnp.sum(jnp.sum(evidence_ref[...], axis=0), axis=1, keepdims=True)
    column = lax.broadcasted_iota(jnp.int32, out_ref.shape, 1)
    row = jnp.zeros(out_ref.shape, jnp.float32)
    for k in range(out_ref.shape[1]):
        row = jnp.where(column == k, total[k : k + 1], row)
    out_ref[...] = row


def last_step(values, evidence):
    return pl.pallas_call(
        last_kernel,
        out_shape=(
            jax.ShapeDtypeStruct((values.shape[0] * values.shape[1], values.shape[2]), jnp.float32),
            jax.ShapeDtypeStruct((1, evidence.shape[1]), jnp.float32),
        ),
        in_specs=[VMEM, VMEM],
        out_specs=(VMEM, VMEM),
        compiler_params=params(),
    )(values, evidence)


def swapped_along_x(shard):
    return lax.ppermute(shard, "bucket", [(b, b ^ 1) for b in range(lax.axis_size("bucket"))])


def shifted_along_y(shard, step):
    count = lax.axis_size("bucket")
    return lax.ppermute(shard, "bucket", [(b, (b - 2 * step) % count) for b in range(count)])


def on_device(spectra, theory, cand, half):
    row_count, bin_count = spectra.shape
    spec_count = lax.axis_size("spec")
    bucket_count = lax.axis_size("bucket")
    per_bucket = theory.shape[0]
    peptides_all = per_bucket * bucket_count
    spec = lax.axis_index("spec").astype(jnp.int32)
    bucket = lax.axis_index("bucket").astype(jnp.int32)
    where = spec.reshape(1), bucket.reshape(1)
    core = (spec % 2).reshape(1)

    inside = [(i, i ^ 1) for i in range(spec_count)]
    outside = [(i, i + 1) for i in range(1, spec_count - 1, 2)]
    outside += [(target, source) for source, target in outside]
    first, last = spectra[:, :SIDE], spectra[:, -SIDE:]
    beside = swapped_along_x(theory)
    above, below = shifted_along_y(theory, 1), shifted_along_y(theory, 3)
    across = shifted_along_y(theory, 2)
    even_core = spec % 2 == 0
    inner = lax.ppermute(jnp.where(even_core, last, first), "spec", inside)
    outer = lax.ppermute(jnp.where(even_core, first, last), "spec", outside)
    above_beside, below_beside = shifted_along_y(beside, 1), shifted_along_y(beside, 3)
    across_beside = swapped_along_x(across)
    processed, cand = windowed(half, where, spectra, inner, outer, cand)
    pieces = [theory, beside, above, above_beside, across, across_beside, below, below_beside]

    own = row_count // spec_count
    keep, send = scored(core, processed, pieces, own)
    got = lax.ppermute(send, "spec", inside)
    chip = (keep + got).astype(jnp.bfloat16)
    groups = [list(range(c, spec_count, 2)) for c in range(2)]
    parts = lax.all_to_all(chip, "spec", 0, 0, axis_index_groups=groups, tiled=True)
    copies = picked_copies(where, parts, cand, spec_count)
    values = lax.all_to_all(copies, "spec", 0, 0, tiled=True)

    share = peptides_all // spec_count
    mean_load = cand.shape[1] * row_count / per_bucket
    evidence = evidence_of(where, values, cand, share, mean_load)
    evidence = lax.all_to_all(
        evidence.reshape(bucket_count, share // bucket_count, cand.shape[1]), "bucket", 0, 0, tiled=True
    )
    cand_scores, totals = last_step(values, evidence)
    return (cand_scores, totals.reshape(-1))


def solution(mesh):
    return jax.shard_map(
        on_device,
        mesh=mesh,
        in_specs=(P("bucket", "spec"), P("bucket", "spec"), P("bucket", None), P("spec")),
        out_specs=(P("bucket", None), P(("spec", "bucket"))),
        check_vma=False,
    )
```

```python
import functools

import jax
import jax.numpy as jnp
from jax import lax
from jax.experimental import pallas as pl
from jax.experimental.pallas import tpu as pltpu
from jax.sharding import PartitionSpec as P

REGION = 512
SIDE = 128
TILE = 256

VMEM = pl.BlockSpec(memory_space=pltpu.VMEM)
SMEM = pl.BlockSpec(memory_space=pltpu.SMEM)


def params():
    return pltpu.CompilerParams(vmem_limit_bytes=16 * 1024 * 1024)


def window_kernel(half_ref, spec_ref, bucket_ref, spectra_ref, inner_ref, outer_ref, cand_ref, out_ref, near_ref, wide_ref):
    near_ref[...] = cand_ref[...]
    bins = spectra_ref.shape[1]
    inner, outer = inner_ref[...], outer_ref[...]
    even_core = spec_ref[0] % 2 == 0
    wide_ref[:, :SIDE] = jnp.where(even_core, outer, inner)
    wide_ref[:, SIDE : SIDE + bins] = spectra_ref[...]
    wide_ref[:, SIDE + bins :] = jnp.where(even_core, inner, outer)
    taken = TILE + 2 * SIDE
    source = lax.broadcasted_iota(jnp.int32, (taken, TILE), 0) - SIDE
    target = lax.broadcasted_iota(jnp.int32, (taken, TILE), 1)
    distance = jnp.abs(source - target)
    for region in range(bins // REGION):
        width = half_ref[region]
        band = jnp.where(distance <= width, 1.0, 0.0).astype(jnp.bfloat16)
        divisor = (2 * width + 1).astype(jnp.float32)
        for tile in range(REGION // TILE):
            at = region * REGION + tile * TILE
            sums = jnp.dot(wide_ref[:, at : at + taken], band, preferred_element_type=jnp.float32)
            middle = wide_ref[:, at + SIDE : at + SIDE + TILE].astype(jnp.float32)
            out_ref[:, at : at + TILE] = (middle - sums / divisor).astype(jnp.bfloat16)


def windowed(half, where, spectra, inner, outer, cand):
    rows, bins = spectra.shape
    return pl.pallas_call(
        window_kernel,
        out_shape=(jax.ShapeDtypeStruct((rows, bins), jnp.bfloat16), jax.ShapeDtypeStruct(cand.shape, cand.dtype)),
        in_specs=[SMEM, SMEM, SMEM, VMEM, VMEM, VMEM, VMEM],
        out_specs=(VMEM, VMEM),
        scratch_shapes=[pltpu.VMEM((rows, bins + 2 * SIDE), jnp.bfloat16)],
        compiler_params=params(),
        cost_estimate=pl.CostEstimate(flops=2 * rows * bins * 512, bytes_accessed=4 * rows * bins, transcendentals=0),
    )(half, *where, spectra, inner, outer, cand)


def score_kernel(core_ref, processed_ref, *refs):
    pieces, keep_ref, send_ref = refs[:-2], refs[-2], refs[-1]
    blocks, own, peptides = keep_ref.shape
    theory = jnp.concatenate([piece[...] for piece in pieces], axis=0)
    scores = lax.dot_general(
        processed_ref[...], theory, (((1,), (1,)), ((), ())), preferred_element_type=jnp.float32
    )
    scores = scores - jnp.mean(scores, axis=1, keepdims=True)
    halves = scores.reshape(blocks, 2, own, peptides)
    even, odd = halves[:, 0], halves[:, 1]
    first = core_ref[0] == 0
    keep_ref[...] = jnp.where(first, even, odd)
    send_ref[...] = jnp.where(first, odd, even)


def scored(core, processed, pieces, own):
    rows, bins = processed.shape
    peptides = sum(piece.shape[0] for piece in pieces)
    half_rows = jax.ShapeDtypeStruct((rows // own // 2, own, peptides), jnp.float32)
    return pl.pallas_call(
        score_kernel,
        out_shape=(half_rows, half_rows),
        in_specs=[SMEM, VMEM] + [VMEM] * len(pieces),
        out_specs=(VMEM, VMEM),
        compiler_params=params(),
        cost_estimate=pl.CostEstimate(
            flops=2 * rows * bins * peptides, bytes_accessed=2 * (rows + peptides) * bins, transcendentals=0
        ),
    )(core, processed, *pieces)


def pick_kernel(spec_ref, bucket_ref, parts_ref, cand_ref, out_ref):
    count, own, peptides = parts_ref.shape
    lanes = cand_ref.shape[1]
    per_bucket = lanes // 2
    rounds = peptides // lanes
    scores = jnp.sum(parts_ref[...].astype(jnp.float32), axis=0)
    centred = scores - jnp.mean(scores, axis=1, keepdims=True)
    spread = jnp.mean(jnp.square(centred), axis=1, keepdims=True)
    first = pl.multiple_of(spec_ref[0] * own, own)
    ids = cand_ref[pl.ds(first, own), :]
    bucket = bucket_ref[0]
    block_of = (ids // lanes - bucket // 2) & (rounds - 1)
    lane_of = (ids & (lanes - 1)) ^ ((bucket & 1) * per_bucket)
    picked = jnp.zeros((own, lanes), jnp.float32)
    for block in range(rounds):
        part = centred[:, block * lanes : (block + 1) * lanes]
        value = jnp.take_along_axis(part, lane_of, axis=1)
        picked = jnp.where(block_of == block, value, picked)
    result = (picked * lax.rsqrt(spread + 1e-06)).astype(out_ref.dtype)
    out_ref[...] = jnp.broadcast_to(result[None], out_ref.shape)


def picked_copies(where, parts, cand, count):
    own = parts.shape[1]
    return pl.pallas_call(
        pick_kernel,
        out_shape=jax.ShapeDtypeStruct((count, own, cand.shape[1]), jnp.bfloat16),
        in_specs=[SMEM, SMEM, VMEM, VMEM],
        out_specs=VMEM,
        compiler_params=params(),
    )(*where, parts, cand)


def evidence_kernel(load, spec_ref, value_ref, cand_ref, out_ref):
    share = out_ref.shape[0]
    rows, lanes = cand_ref.shape
    values = value_ref[...].astype(jnp.float32).reshape(rows, lanes)
    soft = jax.nn.softplus(values)
    ids = cand_ref[...] - spec_ref[0] * share
    for k in range(share):
        kept = jnp.where(ids == k, soft, 0.0)
        out_ref[k : k + 1, :] = jnp.sum(kept, axis=0, keepdims=True) / load


def evidence_of(where, values, cand, share, load):
    return pl.pallas_call(
        functools.partial(evidence_kernel, load),
        out_shape=jax.ShapeDtypeStruct((share, cand.shape[1]), jnp.float32),
        in_specs=[SMEM, VMEM, VMEM],
        out_specs=VMEM,
        compiler_params=params(),
    )(where[0], values, cand)


def last_kernel(value_ref, evidence_ref, wide_ref, out_ref):
    wide_ref[...] = value_ref[...].astype(jnp.float32).reshape(wide_ref.shape)
    total = jnp.sum(jnp.sum(evidence_ref[...], axis=0), axis=1, keepdims=True)
    column = lax.broadcasted_iota(jnp.int32, out_ref.shape, 1)
    row = jnp.zeros(out_ref.shape, jnp.float32)
    for k in range(out_ref.shape[1]):
        row = jnp.where(column == k, total[k : k + 1], row)
    out_ref[...] = row


def last_step(values, evidence):
    return pl.pallas_call(
        last_kernel,
        out_shape=(
            jax.ShapeDtypeStruct((values.shape[0] * values.shape[1], values.shape[2]), jnp.float32),
            jax.ShapeDtypeStruct((1, evidence.shape[1]), jnp.float32),
        ),
        in_specs=[VMEM, VMEM],
        out_specs=(VMEM, VMEM),
        compiler_params=params(),
    )(values, evidence)


def swapped_along_x(shard):
    return lax.ppermute(shard, "bucket", [(b, b ^ 1) for b in range(lax.axis_size("bucket"))])


def shifted_along_y(shard, step):
    count = lax.axis_size("bucket")
    return lax.ppermute(shard, "bucket", [(b, (b - 2 * step) % count) for b in range(count)])


def on_device(spectra, theory, cand, half):
    row_count, bin_count = spectra.shape
    spec_count = lax.axis_size("spec")
    bucket_count = lax.axis_size("bucket")
    per_bucket = theory.shape[0]
    peptides_all = per_bucket * bucket_count
    spec = lax.axis_index("spec").astype(jnp.int32)
    bucket = lax.axis_index("bucket").astype(jnp.int32)
    where = spec.reshape(1), bucket.reshape(1)
    core = (spec % 2).reshape(1)

    inside = [(i, i ^ 1) for i in range(spec_count)]
    outside = [(i, i + 1) for i in range(1, spec_count - 1, 2)]
    outside += [(target, source) for source, target in outside]
    first, last = spectra[:, :SIDE], spectra[:, -SIDE:]
    even_core = spec % 2 == 0
    above = shifted_along_y(theory, 1)
    below = shifted_along_y(theory, 3)
    beside = swapped_along_x(theory)
    across = shifted_along_y(theory, 2)
    inner = lax.ppermute(jnp.where(even_core, last, first), "spec", inside)
    outer = lax.ppermute(jnp.where(even_core, first, last), "spec", outside)
    beside, across, inner = lax.optimization_barrier((beside, across, inner))
    above_beside = shifted_along_y(beside, 1)
    below_beside = shifted_along_y(beside, 3)
    across_beside = swapped_along_x(across)
    processed, cand = windowed(half, where, spectra, inner, outer, cand)
    pieces = [theory, beside, above, above_beside, across, across_beside, below, below_beside]

    own = row_count // spec_count
    keep, send = scored(core, processed, pieces, own)
    got = lax.ppermute(send, "spec", inside)
    chip = (keep + got).astype(jnp.bfloat16)
    groups = [list(range(c, spec_count, 2)) for c in range(2)]
    parts = lax.all_to_all(chip, "spec", 0, 0, axis_index_groups=groups, tiled=True)
    copies = picked_copies(where, parts, cand, spec_count)
    values = lax.all_to_all(copies, "spec", 0, 0, tiled=True)

    share = peptides_all // spec_count
    mean_load = cand.shape[1] * row_count / per_bucket
    evidence = evidence_of(where, values, cand, share, mean_load)
    evidence = lax.all_to_all(
        evidence.reshape(bucket_count, share // bucket_count, cand.shape[1]), "bucket", 0, 0, tiled=True
    )
    cand_scores, totals = last_step(values, evidence)
    return (cand_scores, totals.reshape(-1))


def solution(mesh):
    return jax.shard_map(
        on_device,
        mesh=mesh,
        in_specs=(P("bucket", "spec"), P("bucket", "spec"), P("bucket", None), P("spec")),
        out_specs=(P("bucket", None), P(("spec", "bucket"))),
        check_vma=False,
    )
```

```python
import functools

import jax
import jax.numpy as jnp
from jax import lax
from jax.experimental import pallas as pl
from jax.experimental.pallas import tpu as pltpu
from jax.sharding import PartitionSpec as P

REGION = 512
SIDE = 128
TILE = 256

VMEM = pl.BlockSpec(memory_space=pltpu.VMEM)
SMEM = pl.BlockSpec(memory_space=pltpu.SMEM)


def params():
    return pltpu.CompilerParams(vmem_limit_bytes=16 * 1024 * 1024)


def window_kernel(half_ref, spec_ref, bucket_ref, spectra_ref, inner_ref, outer_ref, cand_ref, out_ref, near_ref, wide_ref):
    near_ref[...] = cand_ref[...]
    bins = spectra_ref.shape[1]
    inner, outer = inner_ref[...], outer_ref[...]
    even_core = spec_ref[0] % 2 == 0
    wide_ref[:, :SIDE] = jnp.where(even_core, outer, inner)
    wide_ref[:, SIDE : SIDE + bins] = spectra_ref[...]
    wide_ref[:, SIDE + bins :] = jnp.where(even_core, inner, outer)
    taken = TILE + 2 * SIDE
    source = lax.broadcasted_iota(jnp.int32, (taken, TILE), 0) - SIDE
    target = lax.broadcasted_iota(jnp.int32, (taken, TILE), 1)
    distance = jnp.abs(source - target)
    for region in range(bins // REGION):
        width = half_ref[region]
        band = jnp.where(distance <= width, 1.0, 0.0).astype(jnp.bfloat16)
        divisor = (2 * width + 1).astype(jnp.float32)
        for tile in range(REGION // TILE):
            at = region * REGION + tile * TILE
            sums = jnp.dot(wide_ref[:, at : at + taken], band, preferred_element_type=jnp.float32)
            middle = wide_ref[:, at + SIDE : at + SIDE + TILE].astype(jnp.float32)
            out_ref[:, at : at + TILE] = (middle - sums / divisor).astype(jnp.bfloat16)


def windowed(half, where, spectra, inner, outer, cand):
    rows, bins = spectra.shape
    return pl.pallas_call(
        window_kernel,
        out_shape=(jax.ShapeDtypeStruct((rows, bins), jnp.bfloat16), jax.ShapeDtypeStruct(cand.shape, cand.dtype)),
        in_specs=[SMEM, SMEM, SMEM, VMEM, VMEM, VMEM, VMEM],
        out_specs=(VMEM, VMEM),
        scratch_shapes=[pltpu.VMEM((rows, bins + 2 * SIDE), jnp.bfloat16)],
        compiler_params=params(),
        cost_estimate=pl.CostEstimate(flops=2 * rows * bins * 512, bytes_accessed=4 * rows * bins, transcendentals=0),
    )(half, *where, spectra, inner, outer, cand)


def product(processed_ref, piece_refs):
    theory = jnp.concatenate([piece[...] for piece in piece_refs], axis=0)
    return lax.dot_general(
        processed_ref[...], theory, (((1,), (1,)), ((), ())), preferred_element_type=jnp.float32
    )


def early_kernel(processed_ref, *refs):
    refs[-1][...] = product(processed_ref, refs[:-1])


def early_scores(processed, pieces):
    rows, bins = processed.shape
    peptides = sum(piece.shape[0] for piece in pieces)
    return pl.pallas_call(
        early_kernel,
        out_shape=jax.ShapeDtypeStruct((rows, peptides), jnp.float32),
        in_specs=[VMEM] * (1 + len(pieces)),
        out_specs=VMEM,
        compiler_params=params(),
        cost_estimate=pl.CostEstimate(
            flops=2 * rows * bins * peptides, bytes_accessed=2 * (rows + peptides) * bins, transcendentals=0
        ),
    )(processed, *pieces)


def score_kernel(core_ref, early_ref, processed_ref, *refs):
    pieces, keep_ref, send_ref = refs[:-2], refs[-2], refs[-1]
    blocks, own, peptides = keep_ref.shape
    scores = jnp.concatenate([early_ref[...], product(processed_ref, pieces)], axis=1)
    scores = scores - jnp.mean(scores, axis=1, keepdims=True)
    halves = scores.reshape(blocks, 2, own, peptides)
    even, odd = halves[:, 0], halves[:, 1]
    first = core_ref[0] == 0
    keep_ref[...] = jnp.where(first, even, odd)
    send_ref[...] = jnp.where(first, odd, even)


def scored(core, early, processed, pieces, own):
    rows, bins = processed.shape
    late = sum(piece.shape[0] for piece in pieces)
    half_rows = jax.ShapeDtypeStruct((rows // own // 2, own, early.shape[1] + late), jnp.float32)
    return pl.pallas_call(
        score_kernel,
        out_shape=(half_rows, half_rows),
        in_specs=[SMEM, VMEM, VMEM] + [VMEM] * len(pieces),
        out_specs=(VMEM, VMEM),
        compiler_params=params(),
        cost_estimate=pl.CostEstimate(
            flops=2 * rows * bins * late, bytes_accessed=2 * (rows + late) * bins, transcendentals=0
        ),
    )(core, early, processed, *pieces)


def pick_kernel(spec_ref, bucket_ref, parts_ref, cand_ref, out_ref):
    count, own, peptides = parts_ref.shape
    lanes = cand_ref.shape[1]
    per_bucket = lanes // 2
    rounds = peptides // lanes
    scores = jnp.sum(parts_ref[...].astype(jnp.float32), axis=0)
    centred = scores - jnp.mean(scores, axis=1, keepdims=True)
    spread = jnp.mean(jnp.square(centred), axis=1, keepdims=True)
    first = pl.multiple_of(spec_ref[0] * own, own)
    ids = cand_ref[pl.ds(first, own), :]
    bucket = bucket_ref[0]
    steps_y = (ids // lanes - bucket // 2) & (rounds - 1)
    steps_x = (ids // per_bucket ^ bucket) & 1
    slot_same = jnp.where(steps_y == 1, 3, jnp.where(steps_y == 3, 4, steps_y))
    slot_beside = jnp.where(steps_y == 0, 1, steps_y + 4)
    column = jnp.where(steps_x == 0, slot_same, slot_beside) * per_bucket + ids % per_bucket
    block_of, lane_of = column // lanes, column % lanes
    picked = jnp.zeros((own, lanes), jnp.float32)
    for block in range(rounds):
        part = centred[:, block * lanes : (block + 1) * lanes]
        value = jnp.take_along_axis(part, lane_of, axis=1)
        picked = jnp.where(block_of == block, value, picked)
    result = (picked * lax.rsqrt(spread + 1e-06)).astype(out_ref.dtype)
    out_ref[...] = jnp.broadcast_to(result[None], out_ref.shape)


def picked_copies(where, parts, cand, count):
    own = parts.shape[1]
    return pl.pallas_call(
        pick_kernel,
        out_shape=jax.ShapeDtypeStruct((count, own, cand.shape[1]), jnp.bfloat16),
        in_specs=[SMEM, SMEM, VMEM, VMEM],
        out_specs=VMEM,
        compiler_params=params(),
    )(*where, parts, cand)


def evidence_kernel(load, spec_ref, value_ref, cand_ref, out_ref):
    share = out_ref.shape[0]
    rows, lanes = cand_ref.shape
    values = value_ref[...].astype(jnp.float32).reshape(rows, lanes)
    soft = jax.nn.softplus(values)
    ids = cand_ref[...] - spec_ref[0] * share
    for k in range(share):
        kept = jnp.where(ids == k, soft, 0.0)
        out_ref[k : k + 1, :] = jnp.sum(kept, axis=0, keepdims=True) / load


def evidence_of(where, values, cand, share, load):
    return pl.pallas_call(
        functools.partial(evidence_kernel, load),
        out_shape=jax.ShapeDtypeStruct((share, cand.shape[1]), jnp.float32),
        in_specs=[SMEM, VMEM, VMEM],
        out_specs=VMEM,
        compiler_params=params(),
    )(where[0], values, cand)


def last_kernel(value_ref, evidence_ref, wide_ref, out_ref):
    wide_ref[...] = value_ref[...].astype(jnp.float32).reshape(wide_ref.shape)
    total = jnp.sum(jnp.sum(evidence_ref[...], axis=0), axis=1, keepdims=True)
    column = lax.broadcasted_iota(jnp.int32, out_ref.shape, 1)
    row = jnp.zeros(out_ref.shape, jnp.float32)
    for k in range(out_ref.shape[1]):
        row = jnp.where(column == k, total[k : k + 1], row)
    out_ref[...] = row


def last_step(values, evidence):
    return pl.pallas_call(
        last_kernel,
        out_shape=(
            jax.ShapeDtypeStruct((values.shape[0] * values.shape[1], values.shape[2]), jnp.float32),
            jax.ShapeDtypeStruct((1, evidence.shape[1]), jnp.float32),
        ),
        in_specs=[VMEM, VMEM],
        out_specs=(VMEM, VMEM),
        compiler_params=params(),
    )(values, evidence)


def swapped_along_x(shard):
    return lax.ppermute(shard, "bucket", [(b, b ^ 1) for b in range(lax.axis_size("bucket"))])


def shifted_along_y(shard, step):
    count = lax.axis_size("bucket")
    return lax.ppermute(shard, "bucket", [(b, (b - 2 * step) % count) for b in range(count)])


def on_device(spectra, theory, cand, half):
    row_count, bin_count = spectra.shape
    spec_count = lax.axis_size("spec")
    bucket_count = lax.axis_size("bucket")
    per_bucket = theory.shape[0]
    peptides_all = per_bucket * bucket_count
    spec = lax.axis_index("spec").astype(jnp.int32)
    bucket = lax.axis_index("bucket").astype(jnp.int32)
    where = spec.reshape(1), bucket.reshape(1)
    core = (spec % 2).reshape(1)

    inside = [(i, i ^ 1) for i in range(spec_count)]
    outside = [(i, i + 1) for i in range(1, spec_count - 1, 2)]
    outside += [(target, source) for source, target in outside]
    first, last = spectra[:, :SIDE], spectra[:, -SIDE:]
    even_core = spec % 2 == 0
    above = shifted_along_y(theory, 1)
    below = shifted_along_y(theory, 3)
    beside = swapped_along_x(theory)
    across = shifted_along_y(theory, 2)
    inner = lax.ppermute(jnp.where(even_core, last, first), "spec", inside)
    outer = lax.ppermute(jnp.where(even_core, first, last), "spec", outside)
    beside, across, inner = lax.optimization_barrier((beside, across, inner))
    above_beside = shifted_along_y(beside, 1)
    below_beside = shifted_along_y(beside, 3)
    across_beside = swapped_along_x(across)
    processed, cand = windowed(half, where, spectra, inner, outer, cand)
    early = early_scores(processed, [theory, beside, across, above])
    pieces = [below, above_beside, across_beside, below_beside]

    own = row_count // spec_count
    keep, send = scored(core, early, processed, pieces, own)
    got = lax.ppermute(send, "spec", inside)
    chip = (keep + got).astype(jnp.bfloat16)
    groups = [list(range(c, spec_count, 2)) for c in range(2)]
    parts = lax.all_to_all(chip, "spec", 0, 0, axis_index_groups=groups, tiled=True)
    copies = picked_copies(where, parts, cand, spec_count)
    values = lax.all_to_all(copies, "spec", 0, 0, tiled=True)

    share = peptides_all // spec_count
    mean_load = cand.shape[1] * row_count / per_bucket
    evidence = evidence_of(where, values, cand, share, mean_load)
    evidence = lax.all_to_all(
        evidence.reshape(bucket_count, share // bucket_count, cand.shape[1]), "bucket", 0, 0, tiled=True
    )
    cand_scores, totals = last_step(values, evidence)
    return (cand_scores, totals.reshape(-1))


def solution(mesh):
    return jax.shard_map(
        on_device,
        mesh=mesh,
        in_specs=(P("bucket", "spec"), P("bucket", "spec"), P("bucket", None), P("spec")),
        out_specs=(P("bucket", None), P(("spec", "bucket"))),
        check_vma=False,
    )
```

```python
import functools

import jax
import jax.numpy as jnp
from jax import lax
from jax.experimental import pallas as pl
from jax.experimental.pallas import tpu as pltpu
from jax.sharding import PartitionSpec as P

REGION = 512
SIDE = 128
TILE = 256

VMEM = pl.BlockSpec(memory_space=pltpu.VMEM)
SMEM = pl.BlockSpec(memory_space=pltpu.SMEM)


def params():
    return pltpu.CompilerParams(vmem_limit_bytes=16 * 1024 * 1024)


def window_kernel(half_ref, spec_ref, bucket_ref, spectra_ref, inner_ref, outer_ref, cand_ref, out_ref, near_ref, wide_ref):
    near_ref[...] = cand_ref[...]
    bins = spectra_ref.shape[1]
    inner, outer = inner_ref[...], outer_ref[...]
    even_core = spec_ref[0] % 2 == 0
    wide_ref[:, :SIDE] = jnp.where(even_core, outer, inner)
    wide_ref[:, SIDE : SIDE + bins] = spectra_ref[...]
    wide_ref[:, SIDE + bins :] = jnp.where(even_core, inner, outer)
    taken = TILE + 2 * SIDE
    source = lax.broadcasted_iota(jnp.int32, (taken, TILE), 0) - SIDE
    target = lax.broadcasted_iota(jnp.int32, (taken, TILE), 1)
    distance = jnp.abs(source - target)
    for region in range(bins // REGION):
        width = half_ref[region]
        band = jnp.where(distance <= width, 1.0, 0.0).astype(jnp.bfloat16)
        divisor = (2 * width + 1).astype(jnp.float32)
        for tile in range(REGION // TILE):
            at = region * REGION + tile * TILE
            sums = jnp.dot(wide_ref[:, at : at + taken], band, preferred_element_type=jnp.float32)
            middle = wide_ref[:, at + SIDE : at + SIDE + TILE].astype(jnp.float32)
            out_ref[:, at : at + TILE] = (middle - sums / divisor).astype(jnp.bfloat16)


def windowed(half, where, spectra, inner, outer, cand):
    rows, bins = spectra.shape
    return pl.pallas_call(
        window_kernel,
        out_shape=(jax.ShapeDtypeStruct((rows, bins), jnp.bfloat16), jax.ShapeDtypeStruct(cand.shape, cand.dtype)),
        in_specs=[SMEM, SMEM, SMEM, VMEM, VMEM, VMEM, VMEM],
        out_specs=(VMEM, VMEM),
        scratch_shapes=[pltpu.VMEM((rows, bins + 2 * SIDE), jnp.bfloat16)],
        compiler_params=params(),
        cost_estimate=pl.CostEstimate(flops=2 * rows * bins * 512, bytes_accessed=4 * rows * bins, transcendentals=0),
    )(half, *where, spectra, inner, outer, cand)


def product(processed_ref, piece_refs):
    theory = jnp.concatenate([piece[...] for piece in piece_refs], axis=0)
    return lax.dot_general(
        processed_ref[...], theory, (((1,), (1,)), ((), ())), preferred_element_type=jnp.float32
    )


def early_kernel(processed_ref, *refs):
    refs[-1][...] = product(processed_ref, refs[:-1])


def early_scores(processed, pieces):
    rows, bins = processed.shape
    peptides = sum(piece.shape[0] for piece in pieces)
    return pl.pallas_call(
        early_kernel,
        out_shape=jax.ShapeDtypeStruct((rows, peptides), jnp.float32),
        in_specs=[VMEM] * (1 + len(pieces)),
        out_specs=VMEM,
        compiler_params=params(),
        cost_estimate=pl.CostEstimate(
            flops=2 * rows * bins * peptides, bytes_accessed=2 * (rows + peptides) * bins, transcendentals=0
        ),
    )(processed, *pieces)


def score_kernel(core_ref, early_ref, processed_ref, *refs):
    pieces, keep_ref, send_ref = refs[:-2], refs[-2], refs[-1]
    blocks, own, peptides = keep_ref.shape
    scores = jnp.concatenate([early_ref[...], product(processed_ref, pieces)], axis=1)
    scores = scores - jnp.mean(scores, axis=1, keepdims=True)
    halves = scores.reshape(blocks, 2, own, peptides)
    even, odd = halves[:, 0], halves[:, 1]
    first = core_ref[0] == 0
    keep_ref[...] = jnp.where(first, even, odd)
    send_ref[...] = jnp.where(first, odd, even).astype(send_ref.dtype)


def scored(core, early, processed, pieces, own):
    rows, bins = processed.shape
    late = sum(piece.shape[0] for piece in pieces)
    half_rows = (rows // own // 2, own, early.shape[1] + late)
    return pl.pallas_call(
        score_kernel,
        out_shape=(jax.ShapeDtypeStruct(half_rows, jnp.float32), jax.ShapeDtypeStruct(half_rows, jnp.bfloat16)),
        in_specs=[SMEM, VMEM, VMEM] + [VMEM] * len(pieces),
        out_specs=(VMEM, VMEM),
        compiler_params=params(),
        cost_estimate=pl.CostEstimate(
            flops=2 * rows * bins * late, bytes_accessed=2 * (rows + late) * bins, transcendentals=0
        ),
    )(core, early, processed, *pieces)


def pick_kernel(spec_ref, bucket_ref, parts_ref, cand_ref, out_ref):
    count, own, peptides = parts_ref.shape
    lanes = cand_ref.shape[1]
    per_bucket = lanes // 2
    rounds = peptides // lanes
    scores = jnp.sum(parts_ref[...].astype(jnp.float32), axis=0)
    centred = scores - jnp.mean(scores, axis=1, keepdims=True)
    spread = jnp.mean(jnp.square(centred), axis=1, keepdims=True)
    first = pl.multiple_of(spec_ref[0] * own, own)
    ids = cand_ref[pl.ds(first, own), :]
    bucket = bucket_ref[0]
    steps_y = (ids // lanes - bucket // 2) & (rounds - 1)
    steps_x = (ids // per_bucket ^ bucket) & 1
    slot_same = jnp.where(steps_y == 1, 3, jnp.where(steps_y == 3, 4, steps_y))
    slot_beside = jnp.where(steps_y == 0, 1, steps_y + 4)
    column = jnp.where(steps_x == 0, slot_same, slot_beside) * per_bucket + ids % per_bucket
    block_of, lane_of = column // lanes, column % lanes
    picked = jnp.zeros((own, lanes), jnp.float32)
    for block in range(rounds):
        part = centred[:, block * lanes : (block + 1) * lanes]
        value = jnp.take_along_axis(part, lane_of, axis=1)
        picked = jnp.where(block_of == block, value, picked)
    result = (picked * lax.rsqrt(spread + 1e-06)).astype(out_ref.dtype)
    out_ref[...] = jnp.broadcast_to(result[None], out_ref.shape)


def picked_copies(where, parts, cand, count):
    own = parts.shape[1]
    return pl.pallas_call(
        pick_kernel,
        out_shape=jax.ShapeDtypeStruct((count, own, cand.shape[1]), jnp.bfloat16),
        in_specs=[SMEM, SMEM, VMEM, VMEM],
        out_specs=VMEM,
        compiler_params=params(),
    )(*where, parts, cand)


def evidence_kernel(load, spec_ref, value_ref, cand_ref, out_ref):
    share = out_ref.shape[0]
    rows, lanes = cand_ref.shape
    values = value_ref[...].astype(jnp.float32).reshape(rows, lanes)
    soft = jax.nn.softplus(values)
    ids = cand_ref[...] - spec_ref[0] * share
    for k in range(share):
        kept = jnp.where(ids == k, soft, 0.0)
        out_ref[k : k + 1, :] = jnp.sum(kept, axis=0, keepdims=True) / load


def evidence_of(where, values, cand, share, load):
    return pl.pallas_call(
        functools.partial(evidence_kernel, load),
        out_shape=jax.ShapeDtypeStruct((share, cand.shape[1]), jnp.float32),
        in_specs=[SMEM, VMEM, VMEM],
        out_specs=VMEM,
        compiler_params=params(),
    )(where[0], values, cand)


def last_kernel(value_ref, evidence_ref, wide_ref, out_ref):
    wide_ref[...] = value_ref[...].astype(jnp.float32).reshape(wide_ref.shape)
    total = jnp.sum(jnp.sum(evidence_ref[...], axis=0), axis=1, keepdims=True)
    column = lax.broadcasted_iota(jnp.int32, out_ref.shape, 1)
    row = jnp.zeros(out_ref.shape, jnp.float32)
    for k in range(out_ref.shape[1]):
        row = jnp.where(column == k, total[k : k + 1], row)
    out_ref[...] = row


def last_step(values, evidence):
    return pl.pallas_call(
        last_kernel,
        out_shape=(
            jax.ShapeDtypeStruct((values.shape[0] * values.shape[1], values.shape[2]), jnp.float32),
            jax.ShapeDtypeStruct((1, evidence.shape[1]), jnp.float32),
        ),
        in_specs=[VMEM, VMEM],
        out_specs=(VMEM, VMEM),
        compiler_params=params(),
    )(values, evidence)


def swapped_along_x(shard):
    return lax.ppermute(shard, "bucket", [(b, b ^ 1) for b in range(lax.axis_size("bucket"))])


def shifted_along_y(shard, step):
    count = lax.axis_size("bucket")
    return lax.ppermute(shard, "bucket", [(b, (b - 2 * step) % count) for b in range(count)])


def on_device(spectra, theory, cand, half):
    row_count, bin_count = spectra.shape
    spec_count = lax.axis_size("spec")
    bucket_count = lax.axis_size("bucket")
    per_bucket = theory.shape[0]
    peptides_all = per_bucket * bucket_count
    spec = lax.axis_index("spec").astype(jnp.int32)
    bucket = lax.axis_index("bucket").astype(jnp.int32)
    where = spec.reshape(1), bucket.reshape(1)
    core = (spec % 2).reshape(1)

    inside = [(i, i ^ 1) for i in range(spec_count)]
    outside = [(i, i + 1) for i in range(1, spec_count - 1, 2)]
    outside += [(target, source) for source, target in outside]
    first, last = spectra[:, :SIDE], spectra[:, -SIDE:]
    even_core = spec % 2 == 0
    above = shifted_along_y(theory, 1)
    below = shifted_along_y(theory, 3)
    beside = swapped_along_x(theory)
    across = shifted_along_y(theory, 2)
    inner = lax.ppermute(jnp.where(even_core, last, first), "spec", inside)
    outer = lax.ppermute(jnp.where(even_core, first, last), "spec", outside)
    beside, across, inner = lax.optimization_barrier((beside, across, inner))
    above_beside = shifted_along_y(beside, 1)
    below_beside = shifted_along_y(beside, 3)
    across_beside = swapped_along_x(across)
    processed, cand = windowed(half, where, spectra, inner, outer, cand)
    early = early_scores(processed, [theory, beside, across, above])
    pieces = [below, above_beside, across_beside, below_beside]

    own = row_count // spec_count
    keep, send = scored(core, early, processed, pieces, own)
    got = lax.ppermute(send, "spec", inside)
    chip = (keep + got.astype(jnp.float32)).astype(jnp.bfloat16)
    groups = [list(range(c, spec_count, 2)) for c in range(2)]
    parts = lax.all_to_all(chip, "spec", 0, 0, axis_index_groups=groups, tiled=True)
    copies = picked_copies(where, parts, cand, spec_count)
    values = lax.all_to_all(copies, "spec", 0, 0, tiled=True)

    share = peptides_all // spec_count
    mean_load = cand.shape[1] * row_count / per_bucket
    evidence = evidence_of(where, values, cand, share, mean_load)
    evidence = lax.all_to_all(
        evidence.reshape(bucket_count, share // bucket_count, cand.shape[1]), "bucket", 0, 0, tiled=True
    )
    cand_scores, totals = last_step(values, evidence)
    return (cand_scores, totals.reshape(-1))


def solution(mesh):
    return jax.shard_map(
        on_device,
        mesh=mesh,
        in_specs=(P("bucket", "spec"), P("bucket", "spec"), P("bucket", None), P("spec")),
        out_specs=(P("bucket", None), P(("spec", "bucket"))),
        check_vma=False,
    )
```
